32 devices in a mesh: grp: 8 (over y, x, core), sub: 4 (over z).
Axes of the slice: x: 2, y: 2, z: 4, core: 2. Of those that a mesh axis runs over, the one named last changes fastest.
Arguments:
- ratings: bfloat16 [32768, 4, 256], P(('grp', 'sub')), may hold values from -6 to 6
- present: int32 [256, 4, 2], P(('grp', 'sub')), may hold values from 0 to 1, as said below
- user_factors: float32 [32768, 256], P(('grp', 'sub')), may hold values from -1.5 to 1.5
- item_factors: float32 [2048, 256], P(('grp', 'sub')), may hold values from -1.5 to 1.5
Outputs:
- users_out: float32 [32768, 256], P(('grp', 'sub'))
- items_out: float32 [2048, 256], P(('grp', 'sub'))
The draws below stay inside these ranges and needn't reach their ends.
Inputs may be any that keep to these rules, and one draw needn't show every extreme that they name: 1 marks a present tile of 128 users by 128 items, 0 an absent one; the share of present tiles differs from device to device.
All inputs are finite; a program needn't handle non-finite values.
Results may differ from the reference program's by a relative error of at most 0.0003.
Values sent between devices are 32-bit elements; how exact they have to be, the bound alone decides.
A program may use at most 64 MiB of HBM per device.

```python
import jax
import jax.numpy as jnp
from jax import lax

K = 256
TILE = 128
TICKS = 4
UDEV = 1024
IBLK = 256
USERS = 32768
ITEMS = 2048
N_GRP = 8
N_SUB = 4


def draw_present(key, part):
    tiles_device = UDEV // TILE
    rows_total = USERS // TILE
    devices_total = rows_total // tiles_device
    level_key, tile_key = jax.random.split(jax.random.fold_in(key, 7))
    levels = jax.random.randint(level_key, (devices_total,), 2, 10)
    owners = jnp.arange(rows_total) // tiles_device
    level_rows = levels[owners]
    rolls = jax.random.randint(tile_key, (rows_total, TICKS, IBLK // TILE), 0, 10)
    marks = (rolls < level_rows[:, None, None]).astype(jnp.int32)
    marks = marks.at[0, 0, 0].set(1)
    marks = marks.at[rows_total - 1, TICKS - 1, IBLK // TILE - 1].set(0)
    return marks


def block_levels(own_key, shape, cuts, low, largest):
    def one(axis_at, shards_of):
        heights = jax.random.uniform(jax.random.fold_in(jax.random.fold_in(own_key, 6), axis_at), (shards_of,), jnp.float32, low / len(cuts), largest / len(cuts))
        return jnp.repeat(jnp.exp(heights), shape[axis_at] // shards_of).reshape((-1,) + (1,) * (len(shape) - axis_at - 1))

    gain = one(*cuts[0])
    for cut in cuts[1:]:
        gain = gain * one(*cut)
    return gain


def bell_draw(key, shape, width, most, shards=(), kind=jnp.bfloat16):
    result = width * jax.random.normal(key, shape, jnp.float32)
    if shards:
        result = result * block_levels(key, shape, shards, -0.22, 0.18)
    return jnp.clip(result, -most, most).astype(kind)


def setup_inputs(seed: int = 0) -> dict:
    streams_of = jax.random.split(jax.random.key(seed), 5)
    ratings = bell_draw(streams_of[0], (USERS, TICKS, IBLK), 1.0, 6.0, ((0, 32),))
    present = draw_present(jax.random.fold_in(streams_of[4], 71), 0)
    user_factors = bell_draw(streams_of[2], (USERS, K), (K ** -0.25), 1.5, ((0, 32),), jnp.float32)
    item_factors = bell_draw(streams_of[3], (ITEMS, K), (K ** -0.25), 1.5, ((0, 32),), jnp.float32)
    return dict(ratings=ratings, present=present, user_factors=user_factors, item_factors=item_factors)


user_rate = 0.05
item_rate = 0.0008
shrink_rate = 0.05


def expand_mask(marks, tile_size):
    tall, wide = marks.shape
    filled = jnp.broadcast_to(marks[:, None, :, None].astype(jnp.float32), (tall, tile_size, wide, tile_size))
    return filled.reshape(tall * tile_size, wide * tile_size)


def update_block(inputs):
    user_part, rating_part, mark_part, item_part = inputs
    filled = expand_mask(mark_part, TILE)
    predicted = jnp.dot(user_part, item_part.T, precision=lax.Precision.HIGHEST, preferred_element_type=jnp.float32)
    errors = filled * (rating_part.astype(jnp.float32) - predicted)
    user_grad = jnp.dot(errors, item_part, precision=lax.Precision.HIGHEST, preferred_element_type=jnp.float32) - shrink_rate * user_part
    item_grad = jnp.dot(errors.T, user_part, precision=lax.Precision.HIGHEST, preferred_element_type=jnp.float32) - shrink_rate * item_part
    return user_part + user_rate * user_grad, item_part + item_rate * item_grad


def reference(ratings, present, user_factors, item_factors):
    groups = N_GRP
    user_rows = user_factors.reshape(groups, N_SUB * UDEV, K)
    rating_rows = ratings.reshape(groups, N_SUB * UDEV, TICKS, IBLK)
    mark_rows = present.reshape(groups, N_SUB * UDEV // TILE, TICKS, IBLK // TILE)
    blocks = item_factors.reshape(groups, IBLK, K)
    for tick_index in range(TICKS):
        user_rows, blocks = lax.map(update_block, (user_rows, rating_rows[:, :, tick_index, :], mark_rows[:, :, tick_index, :], blocks))
        blocks = jnp.roll(blocks, 1, axis=0)
    return user_rows.reshape(USERS, K), blocks.reshape(ITEMS, K)
```

```python
import functools

import jax
import jax.numpy as jnp
from jax import lax
from jax.experimental import pallas as pl
from jax.experimental.pallas import tpu as pltpu
from jax.sharding import PartitionSpec as P

TILE = 128

user_rate = 0.05
item_rate = 0.0008
shrink_rate = 0.05

MESH = pl.DeviceIdType.MESH
NT = ((1,), (1,))
NN = ((1,), (0,))
TN = ((0,), (0,))


def mm(left, right, dims):
    return lax.dot_general(left, right, (dims, ((), ())), preferred_element_type=jnp.float32)


def split(value):
    high = value.astype(jnp.bfloat16)
    low = (value - high.astype(jnp.float32)).astype(jnp.bfloat16)
    return high, low


def kernel(
    n_grp, n_sub, ticks, parts,
    marks, ratings, users, items, users_out, items_out,
    uh, ul, eh, el, vbuf, gbuf, rbuf, stage, vfin,
    init_send, init_recv, rs_send, rs_recv, ag_send, ag_recv, fin_send, fin_recv,
):
    grp = lax.axis_index("grp")
    sub = lax.axis_index("sub")
    after = lax.rem(grp + 1, n_grp)
    before = lax.rem(grp + n_grp - 1, n_grp)
    shard = items.shape[0]
    piece = TILE // n_sub
    user_tiles = users.shape[0] // TILE

    barrier = pltpu.get_barrier_semaphore()
    for k in range(1, n_sub):
        pl.semaphore_signal(barrier, inc=1, device_id=(grp, lax.rem(sub + k, n_sub)), device_id_type=MESH)
    for k in range(n_sub):
        pl.semaphore_signal(barrier, inc=1, device_id=(before, lax.rem(sub + k, n_sub)), device_id_type=MESH)
    pl.semaphore_wait(barrier, 2 * n_sub - 1)

    def init_copy(k):
        peer = lax.rem(sub + k, n_sub)
        return pltpu.make_async_remote_copy(
            src_ref=items,
            dst_ref=vbuf.at[0, pl.ds(sub * shard, shard), :],
            send_sem=init_send.at[k], recv_sem=init_recv.at[k],
            device_id=(grp, peer), device_id_type=MESH,
        )

    for k in range(1, n_sub):
        init_copy(k).start()
    vbuf[0, pl.ds(sub * shard, shard), :] = items[...]
    high, low = split(users[...])
    uh[...] = high
    ul[...] = low
    users_out[...] = users[...]
    for k in range(1, n_sub):
        init_copy(k).wait()

    def rs_copy(t, p, k):
        peer = lax.rem(sub + k, n_sub)
        return pltpu.make_async_remote_copy(
            src_ref=gbuf.at[p, pl.ds(peer * piece, piece), :],
            dst_ref=rbuf.at[t, p, k],
            send_sem=rs_send.at[p, k], recv_sem=rs_recv.at[t, p, k],
            device_id=(grp, peer), device_id_type=MESH,
        )

    def ag_copy(t, p, k):
        peer = lax.rem(sub + k, n_sub)
        return pltpu.make_async_remote_copy(
            src_ref=stage.at[p],
            dst_ref=vbuf.at[t + 1, pl.ds(p * TILE + sub * piece, piece), :],
            send_sem=ag_send.at[p, k], recv_sem=ag_recv.at[t, p, k],
            device_id=(after, peer), device_id_type=MESH,
        )

    def fin_copy(p):
        row = p * TILE + sub * piece
        return pltpu.make_async_remote_copy(
            src_ref=stage.at[p],
            dst_ref=vfin.at[pl.ds(lax.rem(row, shard), piece), :],
            send_sem=fin_send.at[p], recv_sem=fin_recv.at[lax.rem(row, shard) // piece],
            device_id=(after, row // shard), device_id_type=MESH,
        )

    def tick(t, carry):
        for p in range(parts):
            cols = slice(p * TILE, (p + 1) * TILE)

            @pl.when(t > 0)
            def _():
                for k in range(n_sub):
                    ag_copy(t - 1, p, k).wait_recv()

            vh, vl = split(vbuf[t, cols, :])
            pred = mm(uh[...], vh, NT) + mm(uh[...], vl, NT) + mm(ul[...], vh, NT)
            for i in range(user_tiles):
                rows = slice(i * TILE, (i + 1) * TILE)
                mark = marks[(i * ticks + t) * parts + p].astype(jnp.float32)
                error = mark * (ratings[t, rows, cols].astype(jnp.float32) - pred[rows, :])
                high, low = split(error)
                eh[rows, cols] = high
                el[rows, cols] = low
            gbuf[p] = (
                mm(eh[:, cols], uh[...], TN) + mm(eh[:, cols], ul[...], TN) + mm(el[:, cols], uh[...], TN)
            )
            for k in range(1, n_sub):
                rs_copy(t, p, k).start()

        vh, vl = split(vbuf[t])
        grad = mm(eh[...], vh, NN) + mm(eh[...], vl, NN) + mm(el[...], vh, NN)
        old = users_out[...]
        new = old + user_rate * (grad - shrink_rate * old)
        users_out[...] = new
        high, low = split(new)
        uh[...] = high
        ul[...] = low

        for p in range(parts):
            total = gbuf[p, pl.ds(sub * piece, piece), :]
            for k in range(1, n_sub):
                rs_copy(t, p, k).wait_recv()
                total = total + rbuf[t, p, k]
            mine = vbuf[t, pl.ds(p * TILE + sub * piece, piece), :]
            stage[p] = mine + item_rate * (total - shrink_rate * mine)

            @pl.when(t < ticks - 1)
            def _():
                for k in range(n_sub):
                    ag_copy(t, p, k).start()

            @pl.when(t == ticks - 1)
            def _():
                fin_copy(p).start()

        for p in range(parts):
            for k in range(1, n_sub):
                rs_copy(t, p, k).wait_send()

            @pl.when(t < ticks - 1)
            def _():
                for k in range(n_sub):
                    ag_copy(t, p, k).wait_send()

        return carry

    lax.fori_loop(0, ticks, tick, 0)
    for p in range(parts):
        fin_copy(p).wait_send()
    for p in range(parts):
        pltpu.make_async_remote_copy(
            src_ref=stage.at[p], dst_ref=vfin.at[pl.ds(p * piece, piece), :],
            send_sem=fin_send.at[p], recv_sem=fin_recv.at[p],
            device_id=(after, sub), device_id_type=MESH,
        ).wait_recv()
    items_out[...] = vfin[...]


def on_device(n_grp, n_sub, ratings, present, user_factors, item_factors):
    n_users, ticks, block = ratings.shape
    rank = user_factors.shape[1]
    parts = block // TILE
    piece = TILE // n_sub
    shard = item_factors.shape[0]
    f32, bf16 = jnp.float32, jnp.bfloat16
    dma = pltpu.SemaphoreType.DMA
    vmem = pl.BlockSpec(memory_space=pltpu.VMEM)
    return pl.pallas_call(
        functools.partial(kernel, n_grp, n_sub, ticks, parts),
        out_shape=(
            jax.ShapeDtypeStruct(user_factors.shape, f32),
            jax.ShapeDtypeStruct(item_factors.shape, f32),
        ),
        in_specs=[pl.BlockSpec(memory_space=pltpu.SMEM), vmem, vmem, vmem],
        out_specs=(vmem, vmem),
        scratch_shapes=[
            pltpu.VMEM((n_users, rank), bf16),
            pltpu.VMEM((n_users, rank), bf16),
            pltpu.VMEM((n_users, block), bf16),
            pltpu.VMEM((n_users, block), bf16),
            pltpu.VMEM((ticks, block, rank), f32),
            pltpu.VMEM((parts, TILE, rank), f32),
            pltpu.VMEM((ticks, parts, n_sub, piece, rank), f32),
            pltpu.VMEM((parts, piece, rank), f32),
            pltpu.VMEM((shard, rank), f32),
            dma((n_sub,)), dma((n_sub,)),
            dma((parts, n_sub)), dma((ticks, parts, n_sub)),
            dma((parts, n_sub)), dma((ticks, parts, n_sub)),
            dma((parts,)), dma((parts,)),
        ],
        compiler_params=pltpu.CompilerParams(
            collective_id=0, has_side_effects=True, vmem_limit_bytes=48 * 1024 * 1024
        ),
    )(present.reshape(-1), jnp.transpose(ratings, (1, 0, 2)), user_factors, item_factors)


def solution(mesh):
    both = ("grp", "sub")
    return jax.shard_map(
        functools.partial(on_device, mesh.shape["grp"], mesh.shape["sub"]),
        mesh=mesh,
        in_specs=(P(both, None, None), P(both, None, None), P(both, None), P(both, None)),
        out_specs=(P(both, None), P(both, None)),
        check_vma=False,
    )
```

```python
import functools

import jax
import jax.numpy as jnp
from jax import lax
from jax.experimental import pallas as pl
from jax.experimental.pallas import tpu as pltpu
from jax.sharding import PartitionSpec as P

TILE = 128

user_rate = 0.05
item_rate = 0.0008
shrink_rate = 0.05

MESH = pl.DeviceIdType.MESH
NT = ((1,), (1,))
NN = ((1,), (0,))
TN = ((0,), (0,))


def mm(left, right, dims):
    return lax.dot_general(left, right, (dims, ((), ())), preferred_element_type=jnp.float32)


def split(value):
    high = value.astype(jnp.bfloat16)
    low = (value - high.astype(jnp.float32)).astype(jnp.bfloat16)
    return high, low


def kernel(
    n_grp, n_sub, ticks, parts,
    marks, ratings, users, items, users_out, items_out,
    uh, ul, eh, el, vbuf, gbuf, rbuf, stage, vfin,
    init_send, init_recv, rs_send, rs_recv, ag_send, ag_recv, fin_send, fin_recv,
):
    grp = lax.axis_index("grp")
    sub = lax.axis_index("sub")
    after = lax.rem(grp + 1, n_grp)
    before = lax.rem(grp + n_grp - 1, n_grp)
    shard = items.shape[0]
    width = vbuf.shape[1] // parts
    piece = width // n_sub
    items_wide = vbuf.shape[1] // TILE
    span = min(TILE, width)
    user_tiles = users.shape[0] // TILE

    barrier = pltpu.get_barrier_semaphore()
    for k in range(1, n_sub):
        pl.semaphore_signal(barrier, inc=1, device_id=(grp, lax.rem(sub + k, n_sub)), device_id_type=MESH)
    for k in range(n_sub):
        pl.semaphore_signal(barrier, inc=1, device_id=(before, lax.rem(sub + k, n_sub)), device_id_type=MESH)
    pl.semaphore_wait(barrier, 2 * n_sub - 1)

    order = sorted(range(1, n_sub), key=lambda k: (-min(k, n_sub - k), -k))

    def init_copy(k):
        peer = lax.rem(sub + k, n_sub)
        return pltpu.make_async_remote_copy(
            src_ref=items,
            dst_ref=vbuf.at[0, pl.ds(sub * shard, shard), :],
            send_sem=init_send.at[k], recv_sem=init_recv.at[sub],
            device_id=(grp, peer), device_id_type=MESH,
        )

    for k in range(1, n_sub):
        init_copy(k).start()
    vbuf[0, pl.ds(sub * shard, shard), :] = items[...]
    high, low = split(users[...])
    uh[...] = high
    ul[...] = low
    users_out[...] = users[...]

    def rs_copy(t, p, k):
        peer = lax.rem(sub + k, n_sub)
        return pltpu.make_async_remote_copy(
            src_ref=gbuf.at[p, pl.ds(peer * piece, piece), :],
            dst_ref=rbuf.at[t, p, k],
            send_sem=rs_send.at[p, k], recv_sem=rs_recv.at[t, p, k],
            device_id=(grp, peer), device_id_type=MESH,
        )

    def ag_copy(t, p, k):
        peer = lax.rem(sub + k, n_sub)
        return pltpu.make_async_remote_copy(
            src_ref=stage.at[p],
            dst_ref=vbuf.at[t + 1, pl.ds(p * width + sub * piece, piece), :],
            send_sem=ag_send.at[p, k], recv_sem=ag_recv.at[t, p, k],
            device_id=(after, peer), device_id_type=MESH,
        )

    def fin_copy(p):
        row = p * width + sub * piece
        return pltpu.make_async_remote_copy(
            src_ref=stage.at[p],
            dst_ref=vfin.at[pl.ds(lax.rem(row, shard), piece), :],
            send_sem=fin_send.at[p], recv_sem=fin_recv.at[lax.rem(row, shard) // piece],
            device_id=(after, row // shard), device_id_type=MESH,
        )

    def tick(t, carry):
        for p in range(parts):
            cols = slice(p * width, (p + 1) * width)

            @pl.when(t > 0)
            def _():
                for k in range(n_sub):
                    ag_copy(t - 1, p, k).wait_recv()

            for source in range(p * width // shard, (p + 1) * width // shard):
                @pl.when(jnp.logical_and(t == 0, source != sub))
                def _():
                    pltpu.make_async_remote_copy(
                        src_ref=items, dst_ref=vbuf.at[0, pl.ds(source * shard, shard), :],
                        send_sem=init_send.at[0], recv_sem=init_recv.at[source],
                        device_id=(grp, source), device_id_type=MESH,
                    ).wait_recv()

            vh, vl = split(vbuf[t, cols, :])
            pred = mm(uh[...], vh, NT) + mm(uh[...], vl, NT) + mm(ul[...], vh, NT)
            for i in range(user_tiles):
                rows = slice(i * TILE, (i + 1) * TILE)
                for start in range(p * width, (p + 1) * width, span):
                    some = slice(start, start + span)
                    mark = marks[(i * ticks + t) * items_wide + start // TILE].astype(jnp.float32)
                    guess = pred[rows, start - p * width : start - p * width + span]
                    error = mark * (ratings[t, rows, some].astype(jnp.float32) - guess)
                    high, low = split(error)
                    eh[rows, some] = high
                    el[rows, some] = low

            @pl.when(t > 0)
            def _():
                for k in range(1, n_sub):
                    rs_copy(t - 1, p, k).wait_send()

            gbuf[p] = (
                mm(eh[:, cols], uh[...], TN) + mm(eh[:, cols], ul[...], TN) + mm(el[:, cols], uh[...], TN)
            )
            for k in order:
                rs_copy(t, p, k).start()

        vh, vl = split(vbuf[t])
        grad = mm(eh[...], vh, NN) + mm(eh[...], vl, NN) + mm(el[...], vh, NN)
        old = users_out[...]
        new = old + user_rate * (grad - shrink_rate * old)
        users_out[...] = new
        high, low = split(new)
        uh[...] = high
        ul[...] = low

        for p in range(parts):
            total = gbuf[p, pl.ds(sub * piece, piece), :]
            for k in range(1, n_sub):
                rs_copy(t, p, k).wait_recv()
                total = total + rbuf[t, p, k]
            mine = vbuf[t, pl.ds(p * width + sub * piece, piece), :]

            @pl.when(t > 0)
            def _():
                for k in range(n_sub):
                    ag_copy(t - 1, p, k).wait_send()

            stage[p] = mine + item_rate * (total - shrink_rate * mine)

            @pl.when(t < ticks - 1)
            def _():
                for k in [0] + order:
                    ag_copy(t, p, k).start()

            @pl.when(t == ticks - 1)
            def _():
                fin_copy(p).start()

        return carry

    lax.fori_loop(0, ticks, tick, 0)
    for k in range(1, n_sub):
        init_copy(k).wait_send()
    for p in range(parts):
        for k in range(1, n_sub):
            rs_copy(ticks - 1, p, k).wait_send()
        fin_copy(p).wait_send()
    for p in range(parts):
        pltpu.make_async_remote_copy(
            src_ref=stage.at[p], dst_ref=vfin.at[pl.ds(p * piece, piece), :],
            send_sem=fin_send.at[p], recv_sem=fin_recv.at[p],
            device_id=(after, sub), device_id_type=MESH,
        ).wait_recv()
    items_out[...] = vfin[...]


def on_device(n_grp, n_sub, ratings, present, user_factors, item_factors):
    n_users, ticks, block = ratings.shape
    rank = user_factors.shape[1]
    parts = block // TILE
    piece = block // parts // n_sub
    shard = item_factors.shape[0]
    f32, bf16 = jnp.float32, jnp.bfloat16
    dma = pltpu.SemaphoreType.DMA
    vmem = pl.BlockSpec(memory_space=pltpu.VMEM)
    return pl.pallas_call(
        functools.partial(kernel, n_grp, n_sub, ticks, parts),
        out_shape=(
            jax.ShapeDtypeStruct(user_factors.shape, f32),
            jax.ShapeDtypeStruct(item_factors.shape, f32),
        ),
        in_specs=[pl.BlockSpec(memory_space=pltpu.SMEM), vmem, vmem, vmem],
        out_specs=(vmem, vmem),
        scratch_shapes=[
            pltpu.VMEM((n_users, rank), bf16),
            pltpu.VMEM((n_users, rank), bf16),
            pltpu.VMEM((n_users, block), bf16),
            pltpu.VMEM((n_users, block), bf16),
            pltpu.VMEM((ticks, block, rank), f32),
            pltpu.VMEM((parts, block // parts, rank), f32),
            pltpu.VMEM((ticks, parts, n_sub, piece, rank), f32),
            pltpu.VMEM((parts, piece, rank), f32),
            pltpu.VMEM((shard, rank), f32),
            dma((n_sub,)), dma((n_sub,)),
            dma((parts, n_sub)), dma((ticks, parts, n_sub)),
            dma((parts, n_sub)), dma((ticks, parts, n_sub)),
            dma((parts,)), dma((parts,)),
        ],
        compiler_params=pltpu.CompilerParams(
            collective_id=0, has_side_effects=True, vmem_limit_bytes=48 * 1024 * 1024
        ),
    )(present.reshape(-1), jnp.transpose(ratings, (1, 0, 2)), user_factors, item_factors)


def solution(mesh):
    both = ("grp", "sub")
    return jax.shard_map(
        functools.partial(on_device, mesh.shape["grp"], mesh.shape["sub"]),
        mesh=mesh,
        in_specs=(P(both, None, None), P(both, None, None), P(both, None), P(both, None)),
        out_specs=(P(both, None), P(both, None)),
        check_vma=False,
    )
```

```python
import functools

import jax
import jax.numpy as jnp
from jax import lax
from jax.experimental import pallas as pl
from jax.experimental.pallas import tpu as pltpu
from jax.sharding import PartitionSpec as P

TILE = 128

user_rate = 0.05
item_rate = 0.0008
shrink_rate = 0.05

MESH = pl.DeviceIdType.MESH
NT = ((1,), (1,))
NN = ((1,), (0,))
TN = ((0,), (0,))


def mm(left, right, dims):
    return lax.dot_general(left, right, (dims, ((), ())), preferred_element_type=jnp.float32)


def split(value):
    high = value.astype(jnp.bfloat16)
    low = (value - high.astype(jnp.float32)).astype(jnp.bfloat16)
    return high, low


def kernel(
    n_grp, n_sub, ticks, parts,
    marks, ratings, users, items, users_out, items_out,
    uh, ul, eh, el, vbuf, gbuf, rbuf, stage, vfin,
    init_send, init_recv, rs_send, rs_recv, ag_send, ag_recv, fin_send, fin_recv,
):
    grp = lax.axis_index("grp")
    sub = lax.axis_index("sub")
    after = lax.rem(grp + 1, n_grp)
    before = lax.rem(grp + n_grp - 1, n_grp)
    shard = items.shape[0]
    width = vbuf.shape[1] // parts
    piece = width // n_sub
    items_wide = vbuf.shape[1] // TILE
    span = min(TILE, width)
    user_tiles = users.shape[0] // TILE

    barrier = pltpu.get_barrier_semaphore()
    for k in range(1, n_sub):
        pl.semaphore_signal(barrier, inc=1, device_id=(grp, lax.rem(sub + k, n_sub)), device_id_type=MESH)
    for k in range(n_sub):
        pl.semaphore_signal(barrier, inc=1, device_id=(before, lax.rem(sub + k, n_sub)), device_id_type=MESH)
    high, low = split(users[...])
    uh[...] = high
    ul[...] = low
    users_out[...] = users[...]
    pl.semaphore_wait(barrier, 2 * n_sub - 1)

    order = sorted(range(1, n_sub), key=lambda k: (-min(k, n_sub - k), -k))

    def init_copy(k):
        peer = lax.rem(sub + k, n_sub)
        return pltpu.make_async_remote_copy(
            src_ref=items,
            dst_ref=vbuf.at[0, pl.ds(sub * shard, shard), :],
            send_sem=init_send.at[k], recv_sem=init_recv.at[sub],
            device_id=(grp, peer), device_id_type=MESH,
        )

    for k in range(1, n_sub):
        init_copy(k).start()
    vbuf[0, pl.ds(sub * shard, shard), :] = items[...]

    def rs_copy(t, p, k):
        peer = lax.rem(sub + k, n_sub)
        return pltpu.make_async_remote_copy(
            src_ref=gbuf.at[p, pl.ds(peer * piece, piece), :],
            dst_ref=rbuf.at[t, p, k],
            send_sem=rs_send.at[p, k], recv_sem=rs_recv.at[t, p, k],
            device_id=(grp, peer), device_id_type=MESH,
        )

    def ag_copy(t, p, k):
        peer = lax.rem(sub + k, n_sub)
        return pltpu.make_async_remote_copy(
            src_ref=stage.at[p],
            dst_ref=vbuf.at[t + 1, pl.ds(p * width + sub * piece, piece), :],
            send_sem=ag_send.at[p, k], recv_sem=ag_recv.at[t, p, k],
            device_id=(after, peer), device_id_type=MESH,
        )

    def fin_copy(p):
        row = p * width + sub * piece
        return pltpu.make_async_remote_copy(
            src_ref=stage.at[p],
            dst_ref=vfin.at[pl.ds(lax.rem(row, shard), piece), :],
            send_sem=fin_send.at[p], recv_sem=fin_recv.at[lax.rem(row, shard) // piece],
            device_id=(after, row // shard), device_id_type=MESH,
        )

    def tick(t, carry):
        for p in range(parts):
            cols = slice(p * width, (p + 1) * width)

            @pl.when(t > 0)
            def _():
                for k in range(n_sub):
                    ag_copy(t - 1, p, k).wait_recv()

            for source in range(p * width // shard, (p + 1) * width // shard):
                @pl.when(jnp.logical_and(t == 0, source != sub))
                def _():
                    pltpu.make_async_remote_copy(
                        src_ref=items, dst_ref=vbuf.at[0, pl.ds(source * shard, shard), :],
                        send_sem=init_send.at[0], recv_sem=init_recv.at[source],
                        device_id=(grp, source), device_id_type=MESH,
                    ).wait_recv()

            vh, vl = split(vbuf[t, cols, :])
            pred = mm(uh[...], vh, NT) + mm(uh[...], vl, NT) + mm(ul[...], vh, NT)
            for i in range(user_tiles):
                rows = slice(i * TILE, (i + 1) * TILE)
                for start in range(p * width, (p + 1) * width, span):
                    some = slice(start, start + span)
                    mark = marks[(i * ticks + t) * items_wide + start // TILE].astype(jnp.float32)
                    guess = pred[rows, start - p * width : start - p * width + span]
                    error = mark * (ratings[t, rows, some].astype(jnp.float32) - guess)
                    high, low = split(error)
                    eh[rows, some] = high
                    el[rows, some] = low

            @pl.when(t > 0)
            def _():
                for k in range(1, n_sub):
                    rs_copy(t - 1, p, k).wait_send()

            gbuf[p] = (
                mm(eh[:, cols], uh[...], TN) + mm(eh[:, cols], ul[...], TN) + mm(el[:, cols], uh[...], TN)
            )
            for k in order:
                rs_copy(t, p, k).start()

        vh, vl = split(vbuf[t])
        grad = mm(eh[...], vh, NN) + mm(eh[...], vl, NN) + mm(el[...], vh, NN)
        old = users_out[...]
        new = old + user_rate * (grad - shrink_rate * old)
        users_out[...] = new
        high, low = split(new)
        uh[...] = high
        ul[...] = low

        for p in range(parts):
            total = gbuf[p, pl.ds(sub * piece, piece), :]
            for k in range(1, n_sub):
                rs_copy(t, p, k).wait_recv()
                total = total + rbuf[t, p, k]
            mine = vbuf[t, pl.ds(p * width + sub * piece, piece), :]

            @pl.when(t > 0)
            def _():
                for k in range(n_sub):
                    ag_copy(t - 1, p, k).wait_send()

            stage[p] = mine + item_rate * (total - shrink_rate * mine)

            @pl.when(t < ticks - 1)
            def _():
                for k in [0] + order:
                    ag_copy(t, p, k).start()

            @pl.when(t == ticks - 1)
            def _():
                fin_copy(p).start()

        return carry

    lax.fori_loop(0, ticks, tick, 0)
    for k in range(1, n_sub):
        init_copy(k).wait_send()
    for p in range(parts):
        for k in range(1, n_sub):
            rs_copy(ticks - 1, p, k).wait_send()
        fin_copy(p).wait_send()
    for p in range(parts):
        pltpu.make_async_remote_copy(
            src_ref=stage.at[p], dst_ref=vfin.at[pl.ds(p * piece, piece), :],
            send_sem=fin_send.at[p], recv_sem=fin_recv.at[p],
            device_id=(after, sub), device_id_type=MESH,
        ).wait_recv()
    items_out[...] = vfin[...]


def on_device(n_grp, n_sub, ratings, present, user_factors, item_factors):
    n_users, ticks, block = ratings.shape
    rank = user_factors.shape[1]
    parts = block // TILE
    piece = block // parts // n_sub
    shard = item_factors.shape[0]
    f32, bf16 = jnp.float32, jnp.bfloat16
    dma = pltpu.SemaphoreType.DMA
    vmem = pl.BlockSpec(memory_space=pltpu.VMEM)
    return pl.pallas_call(
        functools.partial(kernel, n_grp, n_sub, ticks, parts),
        out_shape=(
            jax.ShapeDtypeStruct(user_factors.shape, f32),
            jax.ShapeDtypeStruct(item_factors.shape, f32),
        ),
        in_specs=[pl.BlockSpec(memory_space=pltpu.SMEM), vmem, vmem, vmem],
        out_specs=(vmem, vmem),
        scratch_shapes=[
            pltpu.VMEM((n_users, rank), bf16),
            pltpu.VMEM((n_users, rank), bf16),
            pltpu.VMEM((n_users, block), bf16),
            pltpu.VMEM((n_users, block), bf16),
            pltpu.VMEM((ticks, block, rank), f32),
            pltpu.VMEM((parts, block // parts, rank), f32),
            pltpu.VMEM((ticks, parts, n_sub, piece, rank), f32),
            pltpu.VMEM((parts, piece, rank), f32),
            pltpu.VMEM((shard, rank), f32),
            dma((n_sub,)), dma((n_sub,)),
            dma((parts, n_sub)), dma((ticks, parts, n_sub)),
            dma((parts, n_sub)), dma((ticks, parts, n_sub)),
            dma((parts,)), dma((parts,)),
        ],
        compiler_params=pltpu.CompilerParams(
            collective_id=0, has_side_effects=True, vmem_limit_bytes=48 * 1024 * 1024
        ),
    )(present.reshape(-1), jnp.transpose(ratings, (1, 0, 2)), user_factors, item_factors)


def solution(mesh):
    both = ("grp", "sub")
    return jax.shard_map(
        functools.partial(on_device, mesh.shape["grp"], mesh.shape["sub"]),
        mesh=mesh,
        in_specs=(P(both, None, None), P(both, None, None), P(both, None), P(both, None)),
        out_specs=(P(both, None), P(both, None)),
        check_vma=False,
    )
```
